32 devices in a mesh: groups: 2 (over y), tensor: 2 (over core), expert: 8 (over z, x).
Axes of the slice: x: 2, y: 2, z: 4, core: 2. Of those that a mesh axis runs over, the one named last changes fastest.
Arguments:
- d_output: bfloat16 [4096, 4096], P(('groups', 'tensor', 'expert')), parts along dimension 0, may hold values from -6 to 6
- w_gate: bfloat16 [8, 4096, 704], P('expert', 'tensor'), may hold values from -0.875 to 0.875
- w_up: bfloat16 [8, 4096, 704], P('expert', 'tensor'), may hold values from -0.875 to 0.875
- w_down: bfloat16 [8, 704, 4096], P('expert', None, 'tensor'), may hold values from -0.0234375 to 0.0234375
- gate_pre: bfloat16 [8, 128, 704], P('expert', 'groups'), parts along dimension 1, may hold values from -6 to 6
- up_pre: bfloat16 [8, 128, 704], P('expert', 'groups'), parts along dimension 1, may hold values from -6 to 6
- gate_scores: float32 [8, 128], P('expert', 'groups'), parts along dimension 1, may hold values from 0.05 to 1
- slot_tokens: int32 [8, 8, 2, 8], P(None, 'expert', None, 'groups'), parts along dimension 3, may hold values from 0 to 127, as said below
- slot_counts: int32 [8, 8, 4], P(None, 'expert', 'groups'), parts along dimension 2, may hold values from 0 to 4, as said below
Outputs:
- d_tokens: bfloat16 [4096, 4096], P(('groups', 'tensor', 'expert')), parts along dimension 0
- d_scores: float32 [8, 128], P('expert', 'groups'), parts along dimension 1
The draws below stay inside these ranges and needn't reach their ends.
There are 2 independent parts, one for each index of `groups`. The reference program is written for one: setup_inputs(seed, part) draws one part's arguments, and reference() takes and returns one part's arrays. A program takes and returns all parts, laid end to end along the dimension named above; an argument that names none is the same for every part. Nothing has to cross between parts.
Inputs may be any that keep to these rules, and one draw needn't show every extreme that they name: `slot_tokens`: the 4 entries of a block are distinct rows of the source device's 128 tokens; entries past the block's count are padding. `slot_counts`: in every draw some expert has all of its blocks full.
All inputs are finite; a program needn't handle non-finite values.
Results may differ from the reference program's by a relative error of at most 0.0051.
Values may be sent and summed in bfloat16 or wider, within the bound.
A program may use at most 64 MiB of HBM per device.

```python
import math
import jax
import jax.numpy as jnp
from jax import lax

D = 4096
H = 704
TOK_DEV = 128
PAIR = 4
EXPERTS = 8
CORES = 2
CAP = 64
TOKENS = 2048


def route_table(key):
    key_order, key_count, key_full = jax.random.split(key, 3)
    ranked = jax.random.randint(key_order, (EXPERTS, EXPERTS, CORES, TOK_DEV), 0, 1 << 20) * TOK_DEV
    ranked = ranked + lax.iota(jnp.int32, TOK_DEV)
    ordered = jnp.argsort(ranked, axis=-1, stable=True)[..., :PAIR].astype(jnp.int32)
    counts = jax.random.randint(key_count, (EXPERTS, EXPERTS, CORES), 0, PAIR + 1)
    full_expert = jax.random.randint(key_full, (), 0, EXPERTS)
    counts = jnp.where(lax.iota(jnp.int32, EXPERTS)[:, None, None] == full_expert, PAIR, counts)
    return (ordered, counts.astype(jnp.int32))


def draw_slot_tokens(key, part):
    ordered, counts = route_table(key)
    return ordered


def draw_slot_counts(key, part):
    ordered, counts = route_table(key)
    return counts


def levels(key, extent, cuts, smallest, high):
    loudness, own = 1.0, jax.random.fold_in(key, 6)
    for dim, blocks in cuts:
        draws = jnp.exp(jax.random.uniform(jax.random.fold_in(own, dim), (blocks,), jnp.float32, smallest / len(cuts), high / len(cuts)))
        loudness = loudness * jnp.repeat(draws, extent[dim] // blocks).reshape([-1 if axis == dim else 1 for axis in range(len(extent))])
    return loudness


def centred(rng, dims, deviation, most, cuts=(), dtype=jnp.bfloat16):
    level = levels(rng, dims, cuts, -0.22, 0.18) if cuts else 1.0
    drawn = jax.random.normal(rng, dims, jnp.float32) * deviation * level
    return jnp.minimum(jnp.maximum(drawn, -most), most).astype(dtype)


def setup_inputs(seed: int = 0, part: int = 0) -> dict:
    arg_keys = jax.random.split(jax.random.key(seed), 10)
    part_splits = jax.random.split(jax.random.fold_in(arg_keys[9], part), 10)
    return {
        "d_output": centred(part_splits[0], (TOKENS, D), 1.0, 6.0, ((0, 16),)),
        "w_gate": centred(arg_keys[1], (EXPERTS, D, H), (H // 16) ** -0.5, 0.875, ((0, 8), (1, 2))),
        "w_up": centred(arg_keys[2], (EXPERTS, D, H), (H // 16) ** -0.5, 0.875, ((0, 8), (1, 2))),
        "w_down": centred(arg_keys[3], (EXPERTS, H, D), (16 * D) ** -0.5, 0.0234375, ((0, 8), (2, 2))),
        "gate_pre": centred(part_splits[4], (EXPERTS, CAP, H), 1.0, 6.0, ((0, 8),)),
        "up_pre": centred(part_splits[5], (EXPERTS, CAP, H), 1.0, 6.0, ((0, 8),)),
        "gate_scores": jnp.clip(jnp.exp(math.log(1.0) - 2.9957323 * jax.random.uniform(part_splits[6], (EXPERTS, CAP), jnp.float32) ** levels(part_splits[6], (EXPERTS, CAP), ((0, 8),), -0.2, 0.2)), 0.05, 1.0),
        "slot_tokens": draw_slot_tokens(jax.random.fold_in(jax.random.fold_in(arg_keys[9], part), 71), part),
        "slot_counts": draw_slot_counts(jax.random.fold_in(jax.random.fold_in(arg_keys[9], part), 71), part),
    }


def reference(d_output, w_gate, w_up, w_down, gate_pre, up_pre, gate_scores, slot_tokens, slot_counts):
    cap = EXPERTS * CORES * PAIR
    source = lax.iota(jnp.int32, CORES)[None, :] * EXPERTS + lax.iota(jnp.int32, EXPERTS)[:, None]
    tokens_of = (source[None, :, :, None] * TOK_DEV + slot_tokens).reshape(EXPERTS, cap).astype(jnp.int32)
    valid = (lax.iota(jnp.int32, PAIR)[None, None, None, :] < slot_counts[..., None]).reshape(EXPERTS, cap)

    def per_expert(summed, expert):
        picked = tokens_of[expert]
        keep_mask = valid[expert]
        slot_rows = jnp.where(keep_mask[:, None], d_output[picked], jnp.zeros((), jnp.bfloat16))
        hidden_grad = jnp.dot(slot_rows, w_down[expert].T, preferred_element_type=jnp.float32)
        gate_val = gate_pre[expert].astype(jnp.float32)
        up_val = up_pre[expert].astype(jnp.float32)
        sigmoid_g = jax.nn.sigmoid(gate_val)
        silu_g = gate_val * sigmoid_g
        scores = jnp.sum(silu_g * up_val * hidden_grad, axis=1)
        d_hidden = gate_scores[expert][:, None] * hidden_grad
        d_gate = (d_hidden * up_val * sigmoid_g * (1.0 + gate_val * (1.0 - sigmoid_g))).astype(jnp.bfloat16)
        d_up = (d_hidden * silu_g).astype(jnp.bfloat16)
        slot_grad = jnp.dot(d_gate, w_gate[expert].T, preferred_element_type=jnp.float32)
        slot_grad = slot_grad + jnp.dot(d_up, w_up[expert].T, preferred_element_type=jnp.float32)
        slot_grad = slot_grad.astype(jnp.bfloat16)
        summed = summed.at[picked].add(slot_grad.astype(jnp.float32))
        return summed, scores

    summed, d_scores = lax.scan(per_expert, jnp.zeros((TOKENS, D), jnp.float32), lax.iota(jnp.int32, EXPERTS))
    return summed.astype(jnp.bfloat16), d_scores
```

```python
import functools

import jax
import jax.numpy as jnp
from jax import lax
from jax.experimental import pallas as pl
from jax.experimental.pallas import tpu as pltpu
from jax.sharding import PartitionSpec as P

MESH = pl.DeviceIdType.MESH
TILE = 16
LANES = 128
F32 = jnp.float32
BF16 = jnp.bfloat16


def far_first(experts):
    offsets = []
    for step in range(experts):
        offset = experts // 2 + ((step + 1) // 2 if step % 2 else -(step // 2))
        offsets.append(offset % experts)
    return [k for k in offsets if k] + [0]


def put(wide, start, count, values):
    rows = wide.shape[0] // (values.shape[1] // LANES)
    for k in range(values.shape[1] // LANES):
        wide[pl.ds(k * rows + start, count, stride=TILE), :] = values[:, k * LANES : (k + 1) * LANES]


def get(wide, start, count, width):
    rows = wide.shape[0] // (width // LANES)
    return jnp.concatenate(
        [wide[pl.ds(k * rows + start, count, stride=TILE), :] for k in range(width // LANES)], axis=1
    )


def narrow(wide, block):
    rows, width = block.shape
    for k in range(width // LANES):
        block[:, k * LANES : (k + 1) * LANES] = wide[k * rows : (k + 1) * rows, :].astype(BF16)


def widen(block, wide):
    rows, width = block.shape
    for k in range(width // LANES):
        wide[k * rows : (k + 1) * rows, :] = block[:, k * LANES : (k + 1) * LANES].astype(F32)


def kernel(
    experts, pair,
    tok_hbm, cnt_hbm, d_hbm, wd_hbm, wg_hbm, wu_hbm, gate_hbm, up_hbm, gs_hbm,
    out_hbm, sc_ref,
    tok, cnt, d_v, wd, wg, wu, gate_b, up_b, gs,
    out_v, pick_f, send1, recv1, rows, hid_send, hid_recv, gate_f, up_f,
    back_f, send2, recv2,
    in_sem, out_sem, s1, r1, sh, rh, s2, r2,
):
    my_t = lax.axis_index("tensor")
    my_e = lax.axis_index("expert")
    n = 2 * experts
    half = wd.shape[2]
    groups = TILE // pair
    piece = half // groups
    tokens = d_v.shape[0]
    order = far_first(experts)

    barrier = pltpu.get_barrier_semaphore()
    peers = []
    for k in order:
        e = lax.rem(my_e + k, experts)
        for dt in (1, 0):
            if k == 0 and dt == 0:
                continue
            peers.append((e, lax.rem(my_t + dt, 2)))
    for e, t in peers:
        pl.semaphore_signal(
            barrier, inc=1, device_id={"tensor": t, "expert": e}, device_id_type=MESH
        )

    loads = []
    for i, (src, dst) in enumerate((
        (tok_hbm, tok), (cnt_hbm, cnt), (d_hbm, d_v), (gate_hbm, gate_b), (up_hbm, up_b),
        (gs_hbm, gs), (wd_hbm, wd), (wg_hbm, wg), (wu_hbm, wu),
    )):
        copy = pltpu.make_async_copy(src, dst, in_sem.at[i])
        copy.start()
        loads.append(copy)

    loads[0].wait()
    loads[1].wait()
    first = my_t == 0
    mine = jnp.where(first, tok[:, 0, 0, :], tok[:, 0, 1, :])
    count = jnp.where(first, cnt[:, 0, 0:1], cnt[:, 0, 1:2])
    lanes = lax.broadcasted_iota(jnp.int32, (experts, tokens), 1)
    parts = []
    for r in range(pair):
        hit = jnp.logical_and(lanes == mine[:, r : r + 1], count > r)
        parts.append(jnp.where(hit, 1.0, 0.0).astype(F32))
    one_hot_f = jnp.concatenate(parts, axis=0)
    one_hot = one_hot_f.astype(BF16)
    one_hot_t = one_hot_f.T.astype(BF16)

    loads[2].wait()
    for t in range(2):
        for c in range(groups):
            cols = slice(t * half + c * piece, t * half + (c + 1) * piece)
            got = jnp.dot(one_hot, d_v[:, cols], preferred_element_type=F32)
            for r in range(pair):
                put(
                    pick_f, t * experts * TILE + c * pair + r, experts,
                    got[r * experts : (r + 1) * experts],
                )
    narrow(pick_f, send1)

    me_flat = my_e * 2 + my_t
    pl.semaphore_wait(barrier, n - 1)

    def first_copy(i, e, t, lands):
        return pltpu.make_async_remote_copy(
            src_ref=send1.at[pl.ds(pl.multiple_of((t * experts + e) * TILE, TILE), TILE)],
            dst_ref=recv1.at[pl.ds(pl.multiple_of(lands * TILE, TILE), TILE)],
            send_sem=s1.at[i], recv_sem=r1.at[lands],
            device_id={"tensor": t, "expert": e}, device_id_type=MESH,
        )

    for i, (e, t) in enumerate(peers):
        first_copy(i, e, t, me_flat).start()
    own = pltpu.make_async_copy(
        send1.at[pl.ds(pl.multiple_of((my_t * experts + my_e) * TILE, TILE), TILE)],
        recv1.at[pl.ds(pl.multiple_of(me_flat * TILE, TILE), TILE)],
        in_sem.at[9],
    )
    own.start()

    for copy in loads[3:6]:
        copy.wait()
    src_id = lax.broadcasted_iota(jnp.int32, (n, n * pair), 0)
    slot_id = lax.broadcasted_iota(jnp.int32, (n, n * pair), 1)
    perm = jnp.concatenate(
        [jnp.where(slot_id == src_id * pair + r, 1.0, 0.0).astype(F32) for r in range(pair)], axis=0
    )
    perm_b = perm.astype(BF16)
    gate_val = jnp.dot(perm_b, gate_b[0], preferred_element_type=F32)
    up_val = jnp.dot(perm_b, up_b[0], preferred_element_type=F32)
    scale = jnp.sum(perm * gs[...], axis=1, keepdims=True)
    sig = jax.nn.sigmoid(gate_val)
    silu = gate_val * sig
    score_w = silu * up_val
    gate_w = up_val * sig * (1.0 + gate_val * (1.0 - sig))
    gate_f[...] = gate_w
    up_f[...] = silu

    loads[6].wait()
    own.wait()
    for i, (e, t) in enumerate(peers):
        first_copy(i, e, t, e * 2 + t).wait_recv()
    widen(recv1, back_f)
    for c in range(groups):
        for r in range(pair):
            rows[r * n : (r + 1) * n, c * piece : (c + 1) * piece] = get(
                back_f, c * pair + r, n, piece
            ).astype(BF16)

    hid_send[...] = lax.dot_general(
        rows[...], wd[0], (((1,), (1,)), ((), ())), preferred_element_type=F32
    )
    swap = pltpu.make_async_remote_copy(
        src_ref=hid_send, dst_ref=hid_recv, send_sem=sh, recv_sem=rh,
        device_id={"tensor": 1 - my_t, "expert": my_e}, device_id_type=MESH,
    )
    swap.start()
    loads[7].wait()
    loads[8].wait()
    swap.wait_recv()
    hidden = hid_send[...] + hid_recv[...]
    scores = jnp.sum(score_w * hidden, axis=1, keepdims=True)
    sc_ref[...] = jnp.sum(perm * scores, axis=0, keepdims=True)
    d_hidden = scale * hidden
    d_gate = (d_hidden * gate_f[...]).astype(BF16)
    d_up = (d_hidden * up_f[...]).astype(BF16)
    for c in range(groups):
        cols = slice(c * piece, (c + 1) * piece)
        part = lax.dot_general(
            d_gate, wg[0, cols, :], (((1,), (1,)), ((), ())), preferred_element_type=F32
        ) + lax.dot_general(
            d_up, wu[0, cols, :], (((1,), (1,)), ((), ())), preferred_element_type=F32
        )
        for r in range(pair):
            put(back_f, c * pair + r, n, part[r * n : (r + 1) * n])
    narrow(back_f, send2)

    my_place = my_t * experts + my_e

    def second_copy(i, e, t, lands):
        return pltpu.make_async_remote_copy(
            src_ref=send2.at[pl.ds(pl.multiple_of((e * 2 + t) * TILE, TILE), TILE)],
            dst_ref=recv2.at[pl.ds(pl.multiple_of(lands * TILE, TILE), TILE)],
            send_sem=s2.at[i], recv_sem=r2.at[lands],
            device_id={"tensor": t, "expert": e}, device_id_type=MESH,
        )

    for i, (e, t) in enumerate(peers):
        second_copy(i, e, t, my_place).start()
    own2 = pltpu.make_async_copy(
        send2.at[pl.ds(pl.multiple_of(me_flat * TILE, TILE), TILE)],
        recv2.at[pl.ds(pl.multiple_of(my_place * TILE, TILE), TILE)],
        in_sem.at[10],
    )
    own2.start()
    own2.wait()
    for i, (e, t) in enumerate(peers):
        second_copy(i, e, t, t * experts + e).wait_recv()
    widen(recv2, pick_f)
    stores = []
    for t in range(2):
        for c in range(groups):
            got = jnp.concatenate(
                [
                    get(pick_f, t * experts * TILE + c * pair + r, experts, piece)
                    for r in range(pair)
                ],
                axis=0,
            ).astype(BF16)
            cols = slice(t * half + c * piece, t * half + (c + 1) * piece)
            out_v[:, cols] = jnp.dot(one_hot_t, got, preferred_element_type=F32).astype(BF16)
            store = pltpu.make_async_copy(
                out_v.at[:, cols], out_hbm.at[:, cols], out_sem.at[t * groups + c]
            )
            store.start()
            stores.append(store)
    for i, (e, t) in enumerate(peers):
        first_copy(i, e, t, me_flat).wait_send()
        second_copy(i, e, t, my_place).wait_send()
    swap.wait_send()
    for store in stores:
        store.wait()


def per_device(
    d_output, w_gate, w_up, w_down, gate_pre, up_pre, gate_scores, slot_tokens, slot_counts
):
    tok_rows, width = d_output.shape
    experts = slot_tokens.shape[0]
    pair = slot_tokens.shape[3]
    hidden = w_down.shape[1]
    half = w_down.shape[2]
    n = 2 * experts
    slots = n * pair
    groups = TILE // pair
    piece = half // groups
    anywhere = pl.BlockSpec(memory_space=pl.ANY)
    dma = pltpu.SemaphoreType.DMA
    return pl.pallas_call(
        functools.partial(kernel, experts, pair),
        out_shape=(
            jax.ShapeDtypeStruct((tok_rows, width), BF16),
            jax.ShapeDtypeStruct((1, slots), F32),
        ),
        in_specs=[anywhere] * 9,
        out_specs=(anywhere, pl.BlockSpec(memory_space=pltpu.VMEM)),
        scratch_shapes=[
            pltpu.VMEM(slot_tokens.shape, jnp.int32),
            pltpu.VMEM(slot_counts.shape, jnp.int32),
            pltpu.VMEM(d_output.shape, BF16),
            pltpu.VMEM(w_down.shape, BF16),
            pltpu.VMEM(w_gate.shape, BF16),
            pltpu.VMEM(w_up.shape, BF16),
            pltpu.VMEM(gate_pre.shape, BF16),
            pltpu.VMEM(up_pre.shape, BF16),
            pltpu.VMEM(gate_scores.shape, F32),
            pltpu.VMEM((tok_rows, width), BF16),
            pltpu.VMEM((n * TILE * piece // LANES, LANES), F32),
            pltpu.VMEM((n * TILE, piece), BF16),
            pltpu.VMEM((n * TILE, piece), BF16),
            pltpu.VMEM((slots, half), BF16),
            pltpu.VMEM((slots, hidden), F32),
            pltpu.VMEM((slots, hidden), F32),
            pltpu.VMEM((slots, hidden), F32),
            pltpu.VMEM((slots, hidden), F32),
            pltpu.VMEM((n * TILE * piece // LANES, LANES), F32),
            pltpu.VMEM((n * TILE, piece), BF16),
            pltpu.VMEM((n * TILE, piece), BF16),
            dma((11,)),
            dma((2 * groups,)),
            dma((n,)),
            dma((n,)),
            dma,
            dma,
            dma((n,)),
            dma((n,)),
        ],
        compiler_params=pltpu.CompilerParams(
            collective_id=0, has_side_effects=True, vmem_limit_bytes=56 * 1024 * 1024
        ),
    )(
        slot_tokens, slot_counts, d_output, w_down, w_gate, w_up, gate_pre, up_pre, gate_scores
    )


def solution(mesh):
    placed = (
        P(("groups", "tensor", "expert"), None),
        P("expert", "tensor", None),
        P("expert", "tensor", None),
        P("expert", None, "tensor"),
        P("expert", "groups", None),
        P("expert", "groups", None),
        P("expert", "groups"),
        P(None, "expert", None, "groups"),
        P(None, "expert", "groups"),
    )
    return jax.shard_map(
        per_device,
        mesh=mesh,
        in_specs=placed,
        out_specs=(P(("groups", "tensor", "expert"), None), P("expert", "groups")),
        check_vma=False,
    )
```

```python
import functools

import jax
import jax.numpy as jnp
from jax import lax
from jax.experimental import pallas as pl
from jax.experimental.pallas import tpu as pltpu
from jax.sharding import PartitionSpec as P

MESH = pl.DeviceIdType.MESH
TILE = 16
LANES = 128
F32 = jnp.float32
BF16 = jnp.bfloat16


def far_first(experts):
    offsets = []
    for step in range(experts):
        offset = experts // 2 + ((step + 1) // 2 if step % 2 else -(step // 2))
        offsets.append(offset % experts)
    return [k for k in offsets if k] + [0]


def put(wide, start, count, values):
    rows = wide.shape[0] // (values.shape[1] // LANES)
    for k in range(values.shape[1] // LANES):
        wide[pl.ds(k * rows + start, count, stride=TILE), :] = values[:, k * LANES : (k + 1) * LANES]


def get(wide, start, count, width):
    rows = wide.shape[0] // (width // LANES)
    return jnp.concatenate(
        [wide[pl.ds(k * rows + start, count, stride=TILE), :] for k in range(width // LANES)], axis=1
    )


def narrow(wide, block):
    rows, width = block.shape
    for k in range(width // LANES):
        block[:, k * LANES : (k + 1) * LANES] = wide[k * rows : (k + 1) * rows, :].astype(BF16)


def widen(block, wide):
    rows, width = block.shape
    for k in range(width // LANES):
        wide[k * rows : (k + 1) * rows, :] = block[:, k * LANES : (k + 1) * LANES].astype(F32)


def picks(my_t, tok, cnt, tokens):
    first = my_t == 0
    mine = jnp.where(first, tok[0, 0], tok[0, 1])
    count = jnp.where(first, cnt[0, 0:1, :], cnt[0, 1:2, :])
    pair, experts = mine.shape
    down = lax.broadcasted_iota(jnp.int32, (tokens, experts), 0)
    parts = []
    for r in range(pair):
        hit = jnp.logical_and(down == mine[r : r + 1, :], count > r)
        parts.append(jnp.where(hit, 1.0, 0.0).astype(F32))
    return jnp.concatenate(parts, axis=1)


def spread_kernel(experts, pair, tok, cnt, back, scores, out_hbm, sc_ref, out_v, wide, out_sem):
    my_t = lax.axis_index("tensor")
    groups = TILE // pair
    tokens, width = out_v.shape
    piece = width // 2 // groups
    one_hot_t = picks(my_t, tok, cnt, tokens).astype(BF16)
    sc_ref[...] = scores[...]
    widen(back, wide)
    stores = []
    for t in range(2):
        for c in range(groups):
            got = jnp.concatenate(
                [
                    get(wide, t * experts * TILE + c * pair + r, experts, piece)
                    for r in range(pair)
                ],
                axis=0,
            ).astype(BF16)
            i = t * groups + c
            cols = slice(i * piece, (i + 1) * piece)
            out_v[:, cols] = jnp.dot(one_hot_t, got, preferred_element_type=F32).astype(BF16)
            store = pltpu.make_async_copy(out_v.at[:, cols], out_hbm.at[:, cols], out_sem.at[i])
            store.start()
            stores.append(store)
    for store in stores:
        store.wait()


def kernel(
    experts, pair,
    tok_hbm, cnt_hbm, d_hbm, wd_hbm, wg_hbm, wu_hbm, gate_hbm, up_hbm, gs_hbm,
    recv2, sc_ref,
    tok, cnt, d_v, wd, wg, wu, gate_b, up_b, gs,
    pick_f, send1, recv1, rows, hid_send, hid_recv, gate_f, up_f,
    back_f, send2,
    in_sem, s1, r1, sh, rh, s2, r2,
):
    my_t = lax.axis_index("tensor")
    my_e = lax.axis_index("expert")
    n = 2 * experts
    half = wd.shape[2]
    groups = TILE // pair
    piece = half // groups
    tokens = d_v.shape[0]
    order = far_first(experts)

    barrier = pltpu.get_barrier_semaphore()
    peers = []
    for k in order:
        e = lax.rem(my_e + k, experts)
        for dt in (1, 0):
            if k == 0 and dt == 0:
                continue
            peers.append((e, lax.rem(my_t + dt, 2)))
    for e, t in peers:
        pl.semaphore_signal(
            barrier, inc=1, device_id={"tensor": t, "expert": e}, device_id_type=MESH
        )

    loads = []
    for i, (src, dst) in enumerate((
        (tok_hbm, tok), (cnt_hbm, cnt), (d_hbm, d_v), (gate_hbm, gate_b), (up_hbm, up_b),
        (gs_hbm, gs), (wd_hbm, wd), (wg_hbm, wg), (wu_hbm, wu),
    )):
        copy = pltpu.make_async_copy(src, dst, in_sem.at[i])
        copy.start()
        loads.append(copy)

    loads[0].wait()
    loads[1].wait()
    first = my_t == 0
    one_hot = picks(my_t, tok, cnt, tokens).T.astype(BF16)

    loads[2].wait()
    for t in range(2):
        for c in range(groups):
            cols = slice(t * half + c * piece, t * half + (c + 1) * piece)
            got = jnp.dot(one_hot, d_v[:, cols], preferred_element_type=F32)
            for r in range(pair):
                put(
                    pick_f, t * experts * TILE + c * pair + r, experts,
                    got[r * experts : (r + 1) * experts],
                )
    narrow(pick_f, send1)

    me_flat = my_e * 2 + my_t
    pl.semaphore_wait(barrier, n - 1)

    def first_copy(i, e, t, lands):
        return pltpu.make_async_remote_copy(
            src_ref=send1.at[pl.ds(pl.multiple_of((t * experts + e) * TILE, TILE), TILE)],
            dst_ref=recv1.at[pl.ds(pl.multiple_of(lands * TILE, TILE), TILE)],
            send_sem=s1.at[i], recv_sem=r1.at[lands],
            device_id={"tensor": t, "expert": e}, device_id_type=MESH,
        )

    for i, (e, t) in enumerate(peers):
        first_copy(i, e, t, me_flat).start()
    own = pltpu.make_async_copy(
        send1.at[pl.ds(pl.multiple_of((my_t * experts + my_e) * TILE, TILE), TILE)],
        recv1.at[pl.ds(pl.multiple_of(me_flat * TILE, TILE), TILE)],
        in_sem.at[9],
    )
    own.start()

    for copy in loads[3:6]:
        copy.wait()
    src_id = lax.broadcasted_iota(jnp.int32, (n, n * pair), 0)
    slot_id = lax.broadcasted_iota(jnp.int32, (n, n * pair), 1)
    perm = jnp.concatenate(
        [jnp.where(slot_id == src_id * pair + r, 1.0, 0.0).astype(F32) for r in range(pair)], axis=0
    )
    perm_b = perm.astype(BF16)
    gate_val = jnp.dot(perm_b, gate_b[0], preferred_element_type=F32)
    up_val = jnp.dot(perm_b, up_b[0], preferred_element_type=F32)
    scale = jnp.sum(perm * gs[...], axis=1, keepdims=True)
    sig = jax.nn.sigmoid(gate_val)
    silu = gate_val * sig
    score_w = silu * up_val
    gate_w = up_val * sig * (1.0 + gate_val * (1.0 - sig))
    gate_f[...] = gate_w
    up_f[...] = silu

    loads[6].wait()
    own.wait()
    for i, (e, t) in enumerate(peers):
        first_copy(i, e, t, e * 2 + t).wait_recv()
    widen(recv1, back_f)
    for c in range(groups):
        for r in range(pair):
            rows[r * n : (r + 1) * n, c * piece : (c + 1) * piece] = get(
                back_f, c * pair + r, n, piece
            ).astype(BF16)

    hid_send[...] = lax.dot_general(
        rows[...], wd[0], (((1,), (1,)), ((), ())), preferred_element_type=F32
    )
    swap = pltpu.make_async_remote_copy(
        src_ref=hid_send, dst_ref=hid_recv, send_sem=sh, recv_sem=rh,
        device_id={"tensor": 1 - my_t, "expert": my_e}, device_id_type=MESH,
    )
    swap.start()
    loads[7].wait()
    loads[8].wait()
    swap.wait_recv()
    hidden = hid_send[...] + hid_recv[...]
    scores = jnp.sum(score_w * hidden, axis=1, keepdims=True)
    sc_ref[...] = jnp.sum(perm * scores, axis=0, keepdims=True)
    d_hidden = scale * hidden
    d_gate = (d_hidden * gate_f[...]).astype(BF16)
    d_up = (d_hidden * up_f[...]).astype(BF16)
    for c in range(groups):
        cols = slice(c * piece, (c + 1) * piece)
        part = lax.dot_general(
            d_gate, wg[0, :, cols], (((1,), (0,)), ((), ())), preferred_element_type=F32
        ) + lax.dot_general(
            d_up, wu[0, :, cols], (((1,), (0,)), ((), ())), preferred_element_type=F32
        )
        for r in range(pair):
            put(back_f, c * pair + r, n, part[r * n : (r + 1) * n])
    narrow(back_f, send2)

    my_place = my_t * experts + my_e

    def second_copy(i, e, t, lands):
        return pltpu.make_async_remote_copy(
            src_ref=send2.at[pl.ds(pl.multiple_of((e * 2 + t) * TILE, TILE), TILE)],
            dst_ref=recv2.at[pl.ds(pl.multiple_of(lands * TILE, TILE), TILE)],
            send_sem=s2.at[i], recv_sem=r2.at[lands],
            device_id={"tensor": t, "expert": e}, device_id_type=MESH,
        )

    for i, (e, t) in enumerate(peers):
        second_copy(i, e, t, my_place).start()
    own2 = pltpu.make_async_copy(
        send2.at[pl.ds(pl.multiple_of(me_flat * TILE, TILE), TILE)],
        recv2.at[pl.ds(pl.multiple_of(my_place * TILE, TILE), TILE)],
        in_sem.at[10],
    )
    own2.start()
    own2.wait()
    for i, (e, t) in enumerate(peers):
        second_copy(i, e, t, t * experts + e).wait_recv()
    for i, (e, t) in enumerate(peers):
        first_copy(i, e, t, me_flat).wait_send()
        second_copy(i, e, t, my_place).wait_send()
    swap.wait_send()

def per_device(
    d_output, w_gate, w_up, w_down, gate_pre, up_pre, gate_scores, slot_tokens, slot_counts
):
    tok_rows, width = d_output.shape
    experts = slot_tokens.shape[0]
    pair = slot_tokens.shape[3]
    hidden = w_down.shape[1]
    half = w_down.shape[2]
    n = 2 * experts
    slots = n * pair
    groups = TILE // pair
    piece = half // groups
    anywhere = pl.BlockSpec(memory_space=pltpu.HBM)
    dma = pltpu.SemaphoreType.DMA
    routes = slot_tokens.transpose(1, 2, 3, 0)
    counts = slot_counts.transpose(1, 2, 0)
    gate_t = w_gate.swapaxes(1, 2)
    up_t = w_up.swapaxes(1, 2)
    block = (n * TILE, piece)
    wide = (n * TILE * piece // LANES, LANES)
    here = pl.BlockSpec(memory_space=pltpu.VMEM)
    back, scores = pl.pallas_call(
        functools.partial(kernel, experts, pair),
        out_shape=(
            jax.ShapeDtypeStruct(block, BF16),
            jax.ShapeDtypeStruct((1, slots), F32),
        ),
        in_specs=[anywhere] * 9,
        out_specs=(here, here),
        scratch_shapes=[
            pltpu.VMEM(routes.shape, jnp.int32),
            pltpu.VMEM(counts.shape, jnp.int32),
            pltpu.VMEM(d_output.shape, BF16),
            pltpu.VMEM(w_down.shape, BF16),
            pltpu.VMEM(gate_t.shape, BF16),
            pltpu.VMEM(up_t.shape, BF16),
            pltpu.VMEM(gate_pre.shape, BF16),
            pltpu.VMEM(up_pre.shape, BF16),
            pltpu.VMEM(gate_scores.shape, F32),
            pltpu.VMEM(wide, F32),
            pltpu.VMEM(block, BF16),
            pltpu.VMEM(block, BF16),
            pltpu.VMEM((slots, half), BF16),
            pltpu.VMEM((slots, hidden), F32),
            pltpu.VMEM((slots, hidden), F32),
            pltpu.VMEM((slots, hidden), F32),
            pltpu.VMEM((slots, hidden), F32),
            pltpu.VMEM(wide, F32),
            pltpu.VMEM(block, BF16),
            dma((11,)),
            dma((n,)),
            dma((n,)),
            dma,
            dma,
            dma((n,)),
            dma((n,)),
        ],
        compiler_params=pltpu.CompilerParams(
            collective_id=0, has_side_effects=True, vmem_limit_bytes=63 * 1024 * 1024
        ),
    )(
        routes, counts, d_output, w_down, gate_t, up_t, gate_pre, up_pre, gate_scores
    )
    return pl.pallas_call(
        functools.partial(spread_kernel, experts, pair),
        out_shape=(
            jax.ShapeDtypeStruct((tok_rows, width), BF16),
            jax.ShapeDtypeStruct((1, slots), F32),
        ),
        in_specs=[here] * 4,
        out_specs=(anywhere, here),
        scratch_shapes=[
            pltpu.VMEM((tok_rows, width), BF16),
            pltpu.VMEM(wide, F32),
            dma((2 * groups,)),
        ],
        compiler_params=pltpu.CompilerParams(vmem_limit_bytes=40 * 1024 * 1024),
    )(routes, counts, back, scores)


def solution(mesh):
    placed = (
        P(("groups", "tensor", "expert"), None),
        P("expert", "tensor", None),
        P("expert", "tensor", None),
        P("expert", None, "tensor"),
        P("expert", "groups", None),
        P("expert", "groups", None),
        P("expert", "groups"),
        P(None, "expert", None, "groups"),
        P(None, "expert", "groups"),
    )
    return jax.shard_map(
        per_device,
        mesh=mesh,
        in_specs=placed,
        out_specs=(P(("groups", "tensor", "expert"), None), P("expert", "groups")),
        check_vma=False,
    )
```

```python
import functools

import jax
import jax.numpy as jnp
from jax import lax
from jax.experimental import pallas as pl
from jax.experimental.pallas import tpu as pltpu
from jax.sharding import PartitionSpec as P

MESH = pl.DeviceIdType.MESH
TILE = 16
LANES = 128
SPLITS = 2
F32 = jnp.float32
BF16 = jnp.bfloat16


def far_first(experts):
    offsets = []
    for step in range(experts):
        offset = experts // 2 + ((step + 1) // 2 if step % 2 else -(step // 2))
        offsets.append(offset % experts)
    return [k for k in offsets if k] + [0]


def put(wide, start, count, values):
    rows = wide.shape[0] // (values.shape[1] // LANES)
    for k in range(values.shape[1] // LANES):
        wide[pl.ds(k * rows + start, count, stride=TILE), :] = values[:, k * LANES : (k + 1) * LANES]


def get(wide, start, count, width):
    rows = wide.shape[0] // (width // LANES)
    return jnp.concatenate(
        [wide[pl.ds(k * rows + start, count, stride=TILE), :] for k in range(width // LANES)], axis=1
    )


def narrow(wide, block, base, count):
    rows, width = block.shape
    for k in range(width // LANES):
        block[base : base + count, k * LANES : (k + 1) * LANES] = wide[
            k * rows + base : k * rows + base + count, :
        ].astype(BF16)


def widen(block, wide, base, count):
    rows, width = block.shape
    for k in range(width // LANES):
        wide[k * rows + base : k * rows + base + count, :] = block[
            base : base + count, k * LANES : (k + 1) * LANES
        ].astype(F32)


def picks(my_t, tok, cnt, tokens):
    first = my_t == 0
    mine = jnp.where(first, tok[0, 0], tok[0, 1])
    count = jnp.where(first, cnt[0, 0:1, :], cnt[0, 1:2, :])
    pair, experts = mine.shape
    down = lax.broadcasted_iota(jnp.int32, (tokens, experts), 0)
    parts = []
    for r in range(pair):
        hit = jnp.logical_and(down == mine[r : r + 1, :], count > r)
        parts.append(jnp.where(hit, 1.0, 0.0).astype(F32))
    return jnp.concatenate(parts, axis=1)


def spread_kernel(experts, pair, tok, cnt, back, scores, out_hbm, sc_ref, out_v, wide, out_sem):
    my_t = lax.axis_index("tensor")
    tokens, width = out_v.shape
    part = pair // SPLITS
    groups = TILE // part
    piece = width // 2 // groups
    held = 2 * experts * TILE
    one_hot_t = picks(my_t, tok, cnt, tokens).astype(BF16)
    sc_ref[...] = scores[...]
    widen(back, wide, 0, SPLITS * held)
    stores = []
    for t in range(2):
        for c in range(groups):
            got = jnp.concatenate(
                [
                    get(
                        wide,
                        r // part * held + t * experts * TILE + c * part + r % part,
                        experts,
                        piece,
                    )
                    for r in range(pair)
                ],
                axis=0,
            ).astype(BF16)
            i = t * groups + c
            cols = slice(i * piece, (i + 1) * piece)
            out_v[:, cols] = jnp.dot(one_hot_t, got, preferred_element_type=F32).astype(BF16)
            store = pltpu.make_async_copy(out_v.at[:, cols], out_hbm.at[:, cols], out_sem.at[i])
            store.start()
            stores.append(store)
    for store in stores:
        store.wait()


def kernel(
    experts, pair,
    tok_hbm, cnt_hbm, d_hbm, wd_hbm, wg_hbm, wu_hbm, gate_hbm, up_hbm, gs_hbm,
    recv2, sc_ref,
    tok, cnt, d_v, wd, wg, wu, gate_b, up_b, gs,
    pick_f, send1, recv1, rows, hid_send, hid_recv, gate_f, up_f, score_f,
    back_f, send2,
    in_sem, s1, r1, sh, rh, s2, r2,
):
    my_t = lax.axis_index("tensor")
    my_e = lax.axis_index("expert")
    n = 2 * experts
    half = wd.shape[2]
    part = pair // SPLITS
    groups = TILE // part
    piece = half // groups
    held = n * TILE
    tokens = d_v.shape[0]
    order = far_first(experts)

    barrier = pltpu.get_barrier_semaphore()
    peers = []
    for k in order:
        e = lax.rem(my_e + k, experts)
        for dt in (1, 0):
            if k == 0 and dt == 0:
                continue
            peers.append((e, lax.rem(my_t + dt, 2)))
    for e, t in peers:
        pl.semaphore_signal(
            barrier, inc=1, device_id={"tensor": t, "expert": e}, device_id_type=MESH
        )

    def load(i, src, dst):
        copy = pltpu.make_async_copy(src, dst, in_sem.at[i])
        copy.start()
        return copy

    routes = [load(0, tok_hbm, tok), load(1, cnt_hbm, cnt)]
    halves = [
        load(2 + t, d_hbm.at[:, t * half : (t + 1) * half], d_v.at[:, t * half : (t + 1) * half])
        for t in range(2)
    ]
    for copy in routes:
        copy.wait()
    one_hot = picks(my_t, tok, cnt, tokens).T.astype(BF16)

    def pick(s):
        chosen = one_hot[s * part * experts : (s + 1) * part * experts]
        for t in range(2):
            if s == 0:
                halves[t].wait()
            for c in range(groups):
                cols = slice(t * half + c * piece, t * half + (c + 1) * piece)
                got = jnp.dot(chosen, d_v[:, cols], preferred_element_type=F32)
                for r in range(part):
                    put(
                        pick_f, s * held + t * experts * TILE + c * part + r, experts,
                        got[r * experts : (r + 1) * experts],
                    )
        narrow(pick_f, send1, s * held, held)

    me_flat = my_e * 2 + my_t
    my_place = my_t * experts + my_e

    def block(ref, s, place):
        return ref.at[pl.ds(pl.multiple_of(s * held + place * TILE, TILE), TILE)]

    def first_copy(s, i, e, t, lands):
        return pltpu.make_async_remote_copy(
            src_ref=block(send1, s, t * experts + e), dst_ref=block(recv1, s, lands),
            send_sem=s1.at[s, i], recv_sem=r1.at[s, lands],
            device_id={"tensor": t, "expert": e}, device_id_type=MESH,
        )

    def second_copy(s, i, e, t, lands):
        return pltpu.make_async_remote_copy(
            src_ref=block(send2, s, e * 2 + t), dst_ref=block(recv2, s, lands),
            send_sem=s2.at[s, i], recv_sem=r2.at[s, lands],
            device_id={"tensor": t, "expert": e}, device_id_type=MESH,
        )

    own1, own2, swaps = [], [], []
    weights = []
    for s in range(SPLITS):
        pick(s)
        if s == 0:
            pl.semaphore_wait(barrier, n - 1)
        for i, (e, t) in enumerate(peers):
            first_copy(s, i, e, t, me_flat).start()
        own1.append(load(9 + s, block(send1, s, my_place), block(recv1, s, me_flat)))
        if s == 0:
            small = [load(4, gate_hbm, gate_b), load(5, up_hbm, up_b), load(6, gs_hbm, gs)]
            weights = [load(7, wd_hbm, wd), load(8, wg_hbm, wg), load(9 + 2 * SPLITS, wu_hbm, wu)]

    for copy in small:
        copy.wait()
    src_id = lax.broadcasted_iota(jnp.int32, (n, n * pair), 0)
    slot_id = lax.broadcasted_iota(jnp.int32, (n, n * pair), 1)
    perm = jnp.concatenate(
        [jnp.where(slot_id == src_id * pair + r, 1.0, 0.0).astype(F32) for r in range(pair)], axis=0
    )
    perm_b = perm.astype(BF16)
    gate_val = jnp.dot(perm_b, gate_b[0], preferred_element_type=F32)
    up_val = jnp.dot(perm_b, up_b[0], preferred_element_type=F32)
    scale = jnp.sum(perm * gs[...], axis=1, keepdims=True)
    sig = jax.nn.sigmoid(gate_val)
    silu = gate_val * sig
    score_f[...] = silu * up_val
    gate_f[...] = scale * (up_val * sig * (1.0 + gate_val * (1.0 - sig)))
    up_f[...] = scale * silu

    weights[0].wait()
    count = part * n
    total = jnp.zeros((1, n * pair), F32)
    for s in range(SPLITS):
        own1[s].wait()
        for i, (e, t) in enumerate(peers):
            first_copy(s, i, e, t, e * 2 + t).wait_recv()
        mine = slice(s * count, (s + 1) * count)
        widen(recv1, back_f, s * held, held)
        for c in range(groups):
            for r in range(part):
                rows[s * count + r * n : s * count + (r + 1) * n, c * piece : (c + 1) * piece] = get(
                    back_f, s * held + c * part + r, n, piece
                ).astype(BF16)
        hid_send[mine] = lax.dot_general(
            rows[mine], wd[0], (((1,), (1,)), ((), ())), preferred_element_type=F32
        )
        swap = pltpu.make_async_remote_copy(
            src_ref=hid_send.at[mine], dst_ref=hid_recv.at[mine],
            send_sem=sh.at[s], recv_sem=rh.at[s],
            device_id={"tensor": 1 - my_t, "expert": my_e}, device_id_type=MESH,
        )
        swap.start()
        swaps.append(swap)
        if s == 0:
            weights[1].wait()
            weights[2].wait()
        swap.wait_recv()
        hidden = hid_send[mine] + hid_recv[mine]
        d_gate = (hidden * gate_f[mine]).astype(BF16)
        d_up = (hidden * up_f[mine]).astype(BF16)
        for c in range(groups):
            cols = slice(c * piece, (c + 1) * piece)
            summed = jnp.dot(
                d_gate, wg[0, :, cols], preferred_element_type=F32
            ) + jnp.dot(d_up, wu[0, :, cols], preferred_element_type=F32)
            for r in range(part):
                put(back_f, s * held + c * part + r, n, summed[r * n : (r + 1) * n])
        narrow(back_f, send2, s * held, held)
        for i, (e, t) in enumerate(peers):
            second_copy(s, i, e, t, my_place).start()
        own2.append(
            load(9 + SPLITS + s, block(send2, s, me_flat), block(recv2, s, my_place))
        )
        scores = jnp.sum(score_f[mine] * hidden, axis=1, keepdims=True)
        total = total + jnp.sum(perm[mine] * scores, axis=0, keepdims=True)
    sc_ref[...] = total
    for s in range(SPLITS):
        for i, (e, t) in enumerate(peers):
            first_copy(s, i, e, t, me_flat).wait_send()
        swaps[s].wait_send()
    for s in range(SPLITS):
        own2[s].wait()
        for i, (e, t) in enumerate(peers):
            second_copy(s, i, e, t, t * experts + e).wait_recv()
            second_copy(s, i, e, t, my_place).wait_send()


def per_device(
    d_output, w_gate, w_up, w_down, gate_pre, up_pre, gate_scores, slot_tokens, slot_counts
):
    tok_rows, width = d_output.shape
    experts = slot_tokens.shape[0]
    pair = slot_tokens.shape[3]
    hidden = w_down.shape[1]
    half = w_down.shape[2]
    n = 2 * experts
    slots = n * pair
    groups = TILE // (pair // SPLITS)
    piece = half // groups
    anywhere = pl.BlockSpec(memory_space=pltpu.HBM)
    dma = pltpu.SemaphoreType.DMA
    routes = slot_tokens.transpose(1, 2, 3, 0)
    counts = slot_counts.transpose(1, 2, 0)
    gate_t = w_gate.swapaxes(1, 2)
    up_t = w_up.swapaxes(1, 2)
    block = (SPLITS * n * TILE, piece)
    wide = (SPLITS * n * TILE * piece // LANES, LANES)
    here = pl.BlockSpec(memory_space=pltpu.VMEM)
    back, scores = pl.pallas_call(
        functools.partial(kernel, experts, pair),
        out_shape=(
            jax.ShapeDtypeStruct(block, BF16),
            jax.ShapeDtypeStruct((1, slots), F32),
        ),
        in_specs=[anywhere] * 9,
        out_specs=(here, here),
        scratch_shapes=[
            pltpu.VMEM(routes.shape, jnp.int32),
            pltpu.VMEM(counts.shape, jnp.int32),
            pltpu.VMEM(d_output.shape, BF16),
            pltpu.VMEM(w_down.shape, BF16),
            pltpu.VMEM(gate_t.shape, BF16),
            pltpu.VMEM(up_t.shape, BF16),
            pltpu.VMEM(gate_pre.shape, BF16),
            pltpu.VMEM(up_pre.shape, BF16),
            pltpu.VMEM(gate_scores.shape, F32),
            pltpu.VMEM(wide, F32),
            pltpu.VMEM(block, BF16),
            pltpu.VMEM(block, BF16),
            pltpu.VMEM((slots, half), BF16),
            pltpu.VMEM((slots, hidden), F32),
            pltpu.VMEM((slots, hidden), F32),
            pltpu.VMEM((slots, hidden), F32),
            pltpu.VMEM((slots, hidden), F32),
            pltpu.VMEM((slots, hidden), F32),
            pltpu.VMEM(wide, F32),
            pltpu.VMEM(block, BF16),
            dma((10 + 2 * SPLITS,)),
            dma((SPLITS, n)),
            dma((SPLITS, n)),
            dma((SPLITS,)),
            dma((SPLITS,)),
            dma((SPLITS, n)),
            dma((SPLITS, n)),
        ],
        compiler_params=pltpu.CompilerParams(
            collective_id=0, has_side_effects=True, vmem_limit_bytes=63 * 1024 * 1024
        ),
    )(
        routes, counts, d_output, w_down, gate_t, up_t, gate_pre, up_pre, gate_scores
    )
    return pl.pallas_call(
        functools.partial(spread_kernel, experts, pair),
        out_shape=(
            jax.ShapeDtypeStruct((tok_rows, width), BF16),
            jax.ShapeDtypeStruct((1, slots), F32),
        ),
        in_specs=[here] * 4,
        out_specs=(anywhere, here),
        scratch_shapes=[
            pltpu.VMEM((tok_rows, width), BF16),
            pltpu.VMEM(wide, F32),
            dma((2 * groups,)),
        ],
        compiler_params=pltpu.CompilerParams(vmem_limit_bytes=40 * 1024 * 1024),
    )(routes, counts, back, scores)


def solution(mesh):
    placed = (
        P(("groups", "tensor", "expert"), None),
        P("expert", "tensor", None),
        P("expert", "tensor", None),
        P("expert", None, "tensor"),
        P("expert", "groups", None),
        P("expert", "groups", None),
        P("expert", "groups"),
        P(None, "expert", None, "groups"),
        P(None, "expert", "groups"),
    )
    return jax.shard_map(
        per_device,
        mesh=mesh,
        in_specs=placed,
        out_specs=(P(("groups", "tensor", "expert"), None), P("expert", "groups")),
        check_vma=False,
    )
```

```python
import functools

import jax
import jax.numpy as jnp
from jax import lax
from jax.experimental import pallas as pl
from jax.experimental.pallas import tpu as pltpu
from jax.sharding import PartitionSpec as P

MESH = pl.DeviceIdType.MESH
TILE = 16
LANES = 128
SPLITS = 1
F32 = jnp.float32
BF16 = jnp.bfloat16


def offsets(experts):
    return [k for k in range(1, experts)] + [0]


def put(wide, start, count, values):
    rows = wide.shape[0] // (values.shape[1] // LANES)
    for k in range(values.shape[1] // LANES):
        wide[pl.ds(k * rows + start, count, stride=TILE), :] = values[:, k * LANES : (k + 1) * LANES]


def get(wide, start, count, width):
    rows = wide.shape[0] // (width // LANES)
    return jnp.concatenate(
        [wide[pl.ds(k * rows + start, count, stride=TILE), :] for k in range(width // LANES)], axis=1
    )


def narrow(wide, block, base, count):
    rows, width = block.shape
    for k in range(width // LANES):
        block[base : base + count, k * LANES : (k + 1) * LANES] = wide[
            k * rows + base : k * rows + base + count, :
        ].astype(BF16)


def widen(block, wide, base, count):
    rows, width = block.shape
    for k in range(width // LANES):
        wide[k * rows + base : k * rows + base + count, :] = block[
            base : base + count, k * LANES : (k + 1) * LANES
        ].astype(F32)


def picks(my_t, tok, cnt, tokens):
    first = my_t == 0
    mine = jnp.where(first, tok[0, 0], tok[0, 1])
    count = jnp.where(first, cnt[0, 0:1, :], cnt[0, 1:2, :])
    pair, experts = mine.shape
    down = lax.broadcasted_iota(jnp.int32, (tokens, experts), 0)
    parts = []
    for r in range(pair):
        hit = jnp.logical_and(down == mine[r : r + 1, :], count > r)
        parts.append(jnp.where(hit, 1.0, 0.0).astype(F32))
    return jnp.concatenate(parts, axis=1)


def spread_kernel(experts, pair, tok, cnt, back, scores, out_hbm, sc_ref, out_v, wide, out_sem):
    my_t = lax.axis_index("tensor")
    tokens, width = out_v.shape
    part = pair // SPLITS
    groups = TILE // part
    piece = width // 2 // groups
    held = 2 * experts * TILE
    one_hot_t = picks(my_t, tok, cnt, tokens).astype(BF16)
    sc_ref[...] = scores[...]
    widen(back, wide, 0, SPLITS * held)
    stores = []
    for t in range(2):
        for c in range(groups):
            got = jnp.concatenate(
                [
                    get(
                        wide,
                        r // part * held + t * experts * TILE + c * part + r % part,
                        experts,
                        piece,
                    )
                    for r in range(pair)
                ],
                axis=0,
            ).astype(BF16)
            i = t * groups + c
            cols = slice(i * piece, (i + 1) * piece)
            out_v[:, cols] = jnp.dot(one_hot_t, got, preferred_element_type=F32).astype(BF16)
            store = pltpu.make_async_copy(out_v.at[:, cols], out_hbm.at[:, cols], out_sem.at[i])
            store.start()
            stores.append(store)
    for store in stores:
        store.wait()


def kernel(
    experts, pair,
    tok_hbm, cnt_hbm, d_hbm, wd_hbm, wg_hbm, wu_hbm, gate_hbm, up_hbm, gs_hbm,
    recv2, sc_ref,
    tok, cnt, d_v, wd, wg, wu, gate_b, up_b, gs,
    pick_f, send1, recv1, rows, hid_send, hid_recv, gate_f, up_f, score_f,
    back_f, send2,
    in_sem, s1, r1, sh, rh, s2, r2,
):
    my_t = lax.axis_index("tensor")
    my_e = lax.axis_index("expert")
    n = 2 * experts
    half = wd.shape[2]
    part = pair // SPLITS
    groups = TILE // part
    piece = half // groups
    held = n * TILE
    tokens = d_v.shape[0]
    order = offsets(experts)

    barrier = pltpu.get_barrier_semaphore()
    peers = []
    for k in order:
        e = lax.rem(my_e + k, experts)
        for dt in (1, 0):
            if k == 0 and dt == 0:
                continue
            peers.append((e, lax.rem(my_t + dt, 2)))
    for e, t in peers:
        pl.semaphore_signal(
            barrier, inc=1, device_id={"tensor": t, "expert": e}, device_id_type=MESH
        )

    def load(i, src, dst):
        copy = pltpu.make_async_copy(src, dst, in_sem.at[i])
        copy.start()
        return copy

    routes = [load(0, tok_hbm, tok), load(1, cnt_hbm, cnt)]
    halves = [
        load(2 + t, d_hbm.at[:, t * half : (t + 1) * half], d_v.at[:, t * half : (t + 1) * half])
        for t in range(2)
    ]
    for copy in routes:
        copy.wait()
    one_hot = picks(my_t, tok, cnt, tokens).T.astype(BF16)

    def pick(s):
        chosen = one_hot[s * part * experts : (s + 1) * part * experts]
        for t in range(2):
            if s == 0:
                halves[t].wait()
            for c in range(groups):
                cols = slice(t * half + c * piece, t * half + (c + 1) * piece)
                got = jnp.dot(chosen, d_v[:, cols], preferred_element_type=F32)
                for r in range(part):
                    put(
                        pick_f, s * held + t * experts * TILE + c * part + r, experts,
                        got[r * experts : (r + 1) * experts],
                    )
        narrow(pick_f, send1, s * held, held)

    me_flat = my_e * 2 + my_t
    my_place = my_t * experts + my_e

    def block(ref, s, place):
        return ref.at[pl.ds(pl.multiple_of(s * held + place * TILE, TILE), TILE)]

    def first_copy(s, i, e, t, lands):
        return pltpu.make_async_remote_copy(
            src_ref=block(send1, s, t * experts + e), dst_ref=block(recv1, s, lands),
            send_sem=s1.at[s, i], recv_sem=r1.at[s, lands],
            device_id={"tensor": t, "expert": e}, device_id_type=MESH,
        )

    def second_copy(s, i, e, t, lands):
        return pltpu.make_async_remote_copy(
            src_ref=block(send2, s, e * 2 + t), dst_ref=block(recv2, s, lands),
            send_sem=s2.at[s, i], recv_sem=r2.at[s, lands],
            device_id={"tensor": t, "expert": e}, device_id_type=MESH,
        )

    own1, own2, swaps = [], [], []
    weights = []
    for s in range(SPLITS):
        pick(s)
        if s == 0:
            pl.semaphore_wait(barrier, n - 1)
        for i, (e, t) in enumerate(peers):
            first_copy(s, i, e, t, me_flat).start()
        own1.append(load(9 + s, block(send1, s, my_place), block(recv1, s, me_flat)))
        if s == 0:
            small = [load(4, gate_hbm, gate_b), load(5, up_hbm, up_b), load(6, gs_hbm, gs)]
            weights = [load(7, wd_hbm, wd), load(8, wg_hbm, wg), load(9 + 2 * SPLITS, wu_hbm, wu)]

    for copy in small:
        copy.wait()
    src_id = lax.broadcasted_iota(jnp.int32, (n, n * pair), 0)
    slot_id = lax.broadcasted_iota(jnp.int32, (n, n * pair), 1)
    perm = jnp.concatenate(
        [jnp.where(slot_id == src_id * pair + r, 1.0, 0.0).astype(F32) for r in range(pair)], axis=0
    )
    perm_b = perm.astype(BF16)
    gate_val = jnp.dot(perm_b, gate_b[0], preferred_element_type=F32)
    up_val = jnp.dot(perm_b, up_b[0], preferred_element_type=F32)
    scale = jnp.sum(perm * gs[...], axis=1, keepdims=True)
    sig = jax.nn.sigmoid(gate_val)
    silu = gate_val * sig
    score_f[...] = silu * up_val
    gate_f[...] = scale * (up_val * sig * (1.0 + gate_val * (1.0 - sig)))
    up_f[...] = scale * silu

    weights[0].wait()
    count = part * n
    total = jnp.zeros((1, n * pair), F32)
    for s in range(SPLITS):
        own1[s].wait()
        for i, (e, t) in enumerate(peers):
            first_copy(s, i, e, t, e * 2 + t).wait_recv()
        mine = slice(s * count, (s + 1) * count)
        widen(recv1, back_f, s * held, held)
        for c in range(groups):
            for r in range(part):
                rows[s * count + r * n : s * count + (r + 1) * n, c * piece : (c + 1) * piece] = get(
                    back_f, s * held + c * part + r, n, piece
                ).astype(BF16)
        hid_send[mine] = lax.dot_general(
            rows[mine], wd[0], (((1,), (1,)), ((), ())), preferred_element_type=F32
        )
        swap = pltpu.make_async_remote_copy(
            src_ref=hid_send.at[mine], dst_ref=hid_recv.at[mine],
            send_sem=sh.at[s], recv_sem=rh.at[s],
            device_id={"tensor": 1 - my_t, "expert": my_e}, device_id_type=MESH,
        )
        swap.start()
        swaps.append(swap)
        if s == 0:
            weights[1].wait()
            weights[2].wait()
        swap.wait_recv()
        hidden = hid_send[mine] + hid_recv[mine]
        d_gate = (hidden * gate_f[mine]).astype(BF16)
        d_up = (hidden * up_f[mine]).astype(BF16)
        for c in range(groups):
            cols = slice(c * piece, (c + 1) * piece)
            summed = jnp.dot(
                d_gate, wg[0, :, cols], preferred_element_type=F32
            ) + jnp.dot(d_up, wu[0, :, cols], preferred_element_type=F32)
            for r in range(part):
                put(back_f, s * held + c * part + r, n, summed[r * n : (r + 1) * n])
        narrow(back_f, send2, s * held, held)
        for i, (e, t) in enumerate(peers):
            second_copy(s, i, e, t, my_place).start()
        own2.append(
            load(9 + SPLITS + s, block(send2, s, me_flat), block(recv2, s, my_place))
        )
        scores = jnp.sum(score_f[mine] * hidden, axis=1, keepdims=True)
        total = total + jnp.sum(perm[mine] * scores, axis=0, keepdims=True)
    sc_ref[...] = total
    for s in range(SPLITS):
        for i, (e, t) in enumerate(peers):
            first_copy(s, i, e, t, me_flat).wait_send()
        swaps[s].wait_send()
    for s in range(SPLITS):
        own2[s].wait()
        for i, (e, t) in enumerate(peers):
            second_copy(s, i, e, t, t * experts + e).wait_recv()
            second_copy(s, i, e, t, my_place).wait_send()


def per_device(
    d_output, w_gate, w_up, w_down, gate_pre, up_pre, gate_scores, slot_tokens, slot_counts
):
    tok_rows, width = d_output.shape
    experts = slot_tokens.shape[0]
    pair = slot_tokens.shape[3]
    hidden = w_down.shape[1]
    half = w_down.shape[2]
    n = 2 * experts
    slots = n * pair
    groups = TILE // (pair // SPLITS)
    piece = half // groups
    anywhere = pl.BlockSpec(memory_space=pltpu.HBM)
    dma = pltpu.SemaphoreType.DMA
    routes = slot_tokens.transpose(1, 2, 3, 0)
    counts = slot_counts.transpose(1, 2, 0)
    gate_t = w_gate.swapaxes(1, 2)
    up_t = w_up.swapaxes(1, 2)
    block = (SPLITS * n * TILE, piece)
    wide = (SPLITS * n * TILE * piece // LANES, LANES)
    here = pl.BlockSpec(memory_space=pltpu.VMEM)
    back, scores = pl.pallas_call(
        functools.partial(kernel, experts, pair),
        out_shape=(
            jax.ShapeDtypeStruct(block, BF16),
            jax.ShapeDtypeStruct((1, slots), F32),
        ),
        in_specs=[anywhere] * 9,
        out_specs=(here, here),
        scratch_shapes=[
            pltpu.VMEM(routes.shape, jnp.int32),
            pltpu.VMEM(counts.shape, jnp.int32),
            pltpu.VMEM(d_output.shape, BF16),
            pltpu.VMEM(w_down.shape, BF16),
            pltpu.VMEM(gate_t.shape, BF16),
            pltpu.VMEM(up_t.shape, BF16),
            pltpu.VMEM(gate_pre.shape, BF16),
            pltpu.VMEM(up_pre.shape, BF16),
            pltpu.VMEM(gate_scores.shape, F32),
            pltpu.VMEM(wide, F32),
            pltpu.VMEM(block, BF16),
            pltpu.VMEM(block, BF16),
            pltpu.VMEM((slots, half), BF16),
            pltpu.VMEM((slots, hidden), F32),
            pltpu.VMEM((slots, hidden), F32),
            pltpu.VMEM((slots, hidden), F32),
            pltpu.VMEM((slots, hidden), F32),
            pltpu.VMEM((slots, hidden), F32),
            pltpu.VMEM(wide, F32),
            pltpu.VMEM(block, BF16),
            dma((10 + 2 * SPLITS,)),
            dma((SPLITS, n)),
            dma((SPLITS, n)),
            dma((SPLITS,)),
            dma((SPLITS,)),
            dma((SPLITS, n)),
            dma((SPLITS, n)),
        ],
        compiler_params=pltpu.CompilerParams(
            collective_id=0, has_side_effects=True, vmem_limit_bytes=63 * 1024 * 1024
        ),
    )(
        routes, counts, d_output, w_down, gate_t, up_t, gate_pre, up_pre, gate_scores
    )
    return pl.pallas_call(
        functools.partial(spread_kernel, experts, pair),
        out_shape=(
            jax.ShapeDtypeStruct((tok_rows, width), BF16),
            jax.ShapeDtypeStruct((1, slots), F32),
        ),
        in_specs=[here] * 4,
        out_specs=(anywhere, here),
        scratch_shapes=[
            pltpu.VMEM((tok_rows, width), BF16),
            pltpu.VMEM(wide, F32),
            dma((2 * groups,)),
        ],
        compiler_params=pltpu.CompilerParams(vmem_limit_bytes=63 * 1024 * 1024),
    )(routes, counts, back, scores)


def solution(mesh):
    placed = (
        P(("groups", "tensor", "expert"), None),
        P("expert", "tensor", None),
        P("expert", "tensor", None),
        P("expert", None, "tensor"),
        P("expert", "groups", None),
        P("expert", "groups", None),
        P("expert", "groups"),
        P(None, "expert", None, "groups"),
        P(None, "expert", "groups"),
    )
    return jax.shard_map(
        per_device,
        mesh=mesh,
        in_specs=placed,
        out_specs=(P(("groups", "tensor", "expert"), None), P("expert", "groups")),
        check_vma=False,
    )
```
